32 devices in a mesh: grp: 2 (over y), req: 4 (over z), hid: 2 (over x), kv: 2 (over core).
Axes of the slice: x: 2, y: 2, z: 4, core: 2. Of those that a mesh axis runs over, the one named last changes fastest.
Arguments:
- residual: bfloat16 [256, 3072], P(('grp', 'req', 'hid', 'kv')), parts along dimension 0, may hold values from -6 to 6
- queries: bfloat16 [16, 16, 3072], P(('grp', 'req', 'hid'), None, 'kv'), parts along dimension 0, may hold values from -220 to 220
- tree_row_keys: bfloat16 [16, 16, 512], P(('grp', 'req', 'hid'), None, 'kv'), parts along dimension 0, may hold values from -6 to 6
- tree_row_values: bfloat16 [16, 16, 512], P(('grp', 'req', 'hid'), None, 'kv'), parts along dimension 0, may hold values from -6 to 6
- cache_keys: bfloat16 [16, 1024, 512], P(('grp', 'req', 'hid'), None, 'kv'), parts along dimension 0, may hold values from -6 to 6
- stored_values: bfloat16 [16, 1024, 512], P(('grp', 'req', 'hid'), None, 'kv'), parts along dimension 0, may hold values from -6 to 6
- cache_lengths: int32 [16], P(('grp', 'req', 'hid')), parts along dimension 0, may hold values from 128 to 1024, as said below
- tree_sizes: int32 [16], P(('grp', 'req', 'hid')), parts along dimension 0, may hold values from 1 to 16, as said below
- tree_mask: int32 [16, 16, 16], P(('grp', 'req', 'hid')), parts along dimension 0, may hold values from 0 to 1, as said below
- routes: int32 [256, 2], P(('grp', 'req', 'hid', 'kv')), parts along dimension 0, may hold values from 0 to 3, all different within a row; in each aligned block of 8 rows (0 to 7, 8 to 15, ...) at most 5 rows name the same one
- norm_gain: bfloat16 [3072], replicated, may hold values from 0.099609375 to 1.8984375
- router: bfloat16 [3072, 4], replicated, may hold values from -0.109375 to 0.109375
- gate_weight: bfloat16 [3072, 32768], P('kv', ('req', 'hid')), may hold values from -0.109375 to 0.109375
- up_weight: bfloat16 [3072, 32768], P('kv', ('req', 'hid')), may hold values from -0.109375 to 0.109375
- down_weight: bfloat16 [32768, 3072], P(('req', 'hid'), 'kv'), may hold values from -0.0625 to 0.0625
Outputs:
- expert_mix: bfloat16 [256, 3072], P(('grp', 'req', 'hid', 'kv')), parts along dimension 0
- hidden_state: bfloat16 [256, 3072], P(('grp', 'req', 'hid', 'kv')), parts along dimension 0
The draws below stay inside these ranges and needn't reach their ends.
There are 2 independent parts, one for each index of `grp`. The reference program is written for one: setup_inputs(seed, part) draws one part's arguments, and reference() takes and returns one part's arrays. A program takes and returns all parts, laid end to end along the dimension named above; an argument that names none is the same for every part. Nothing has to cross between parts.
Inputs may be any that keep to these rules, and one draw needn't show every extreme that they name: `cache_lengths`: some request has exactly 1024 live slots. `tree_sizes`: some request has exactly 16 live rows. tree_mask[b, t, u] is 1 exactly when u is t or an ancestor of t in request b's tree; every row's parent has a lower index; row 0 is the root. `routes`: the two experts of a row differ; within each aligned block of 8 rows (the rows of one device), no expert is named by more than 5 rows.
All inputs are finite; a program needn't handle non-finite values.
Results may differ from the reference program's by a relative error of at most 0.009.
Values may be sent and summed in bfloat16 or wider, within the bound.
A program may use at most 256 MiB of HBM per device.

```python
import math
import jax
import jax.numpy as jnp
import numpy as np
from jax import lax

HEAD_SIZE = 128
QUERY_HEADS = 24
KEY_HEADS = 4
D = 3072
FF = 8192
EXPERTS = 4
TREE_ROWS = 16
CACHE_SLOTS = 1024
REQUEST_COUNT = 8
TOKENS = 128
ROWS_DEV = 8
CAP = 5
N_REQ = 4
N_HID = 2


def shared_keys(key):
    return jnp.clip(jax.random.normal(key, (REQUEST_COUNT, CACHE_SLOTS, KEY_HEADS * HEAD_SIZE), jnp.float32), -6.0, 6.0)


def draw_cache_keys(key, part):
    base_offset = shared_keys(key)
    return base_offset.astype(jnp.bfloat16)


def draw_queries(key, part):
    key = jax.random.fold_in(key, 5)
    first = jax.random.fold_in(key, 0)
    values = jnp.clip(jax.random.normal(first, (REQUEST_COUNT, TREE_ROWS, QUERY_HEADS * HEAD_SIZE), jnp.float32), -6.0, 6.0)
    return values.astype(jnp.bfloat16)


def draw_cache_lengths(key, part):
    key = jax.random.fold_in(key, 7)
    first, second = jax.random.split(key)
    lengths = jax.random.randint(first, (REQUEST_COUNT,), CACHE_SLOTS // 8, CACHE_SLOTS + 1, jnp.int32)
    longest = jax.random.randint(second, (), 0, REQUEST_COUNT, jnp.int32)
    return jnp.where(jnp.arange(REQUEST_COUNT, dtype=jnp.int32) == longest, CACHE_SLOTS, lengths).astype(jnp.int32)


def draw_tree_sizes(key, part):
    key = jax.random.fold_in(key, 8)
    first, second = jax.random.split(key)
    sizes = jax.random.randint(first, (REQUEST_COUNT,), 1, TREE_ROWS + 1, jnp.int32)
    largest = jax.random.randint(second, (), 0, REQUEST_COUNT, jnp.int32)
    return jnp.where(jnp.arange(REQUEST_COUNT, dtype=jnp.int32) == largest, TREE_ROWS, sizes).astype(jnp.int32)


def draw_tree_mask(key, part):
    key = jax.random.fold_in(key, 9)
    spread = jax.random.randint(key, (REQUEST_COUNT, TREE_ROWS), 0, 1 << 20, jnp.int32)
    positions = jnp.arange(TREE_ROWS, dtype=jnp.int32)
    parents = spread % jnp.maximum(positions, 1)[None, :]
    identity = (positions[:, None] == positions[None, :]).astype(jnp.int32)
    requests = jnp.arange(REQUEST_COUNT, dtype=jnp.int32)

    def step(position, mask):
        inherited = mask[requests, parents[:, position]]
        own_row = jnp.maximum(inherited, (positions == position).astype(jnp.int32)[None, :])
        return lax.dynamic_update_slice_in_dim(mask, own_row[:, None, :], position, axis=1)
    start = jnp.broadcast_to(identity[None], (REQUEST_COUNT, TREE_ROWS, TREE_ROWS))
    return lax.fori_loop(1, TREE_ROWS, step, start).astype(jnp.int32)


def block_scale(stream_key, shape, shards, least, top_value):
    def one(dim, shards_of):
        steps = jax.random.uniform(jax.random.fold_in(jax.random.fold_in(stream_key, 6), dim), (shards_of,), jnp.float32, least / len(shards), top_value / len(shards))
        return jnp.repeat(jnp.exp(steps), shape[dim] // shards_of).reshape((-1,) + (1,) * (len(shape) - dim - 1))

    factor_of = one(*shards[0])
    for cut in shards[1:]:
        factor_of = factor_of * one(*cut)
    return factor_of


def deal_out(own_key, own, number, rows, number_of, top, limit, slope):
    sequence = jax.random.permutation(own_key, number_of)
    heavy_load, ordinary = load_shares(number_of, rows * top, limit, slope, True), load_shares(number_of, rows * top, limit, slope, False)
    places = jnp.arange(number_of)

    def named(sizes, turn):
        used = int((sizes > 0).sum())
        fixed = max(1, used // 4)
        passed = fixed + (places - fixed + turn * (used - fixed)) % max(1, number_of - fixed)
        return jnp.zeros((number_of,), jnp.int32).at[sequence[jnp.where(places < fixed, places, passed)]].set(jnp.asarray(sizes, jnp.int32))

    sizes = jnp.where(number % 4 == 0, named(heavy_load, number // 4), named(ordinary, number - number // 4 - 1))
    mixed = jax.random.permutation(jax.random.fold_in(own, 3), number_of)
    donor, receiver = mixed[0:number_of // 2 * 2:2], mixed[1:number_of // 2 * 2:2]
    slack = jnp.minimum(sizes[donor] - 1, limit - sizes[receiver]) // 2
    slack = jnp.where((donor == sequence[0]) | (receiver == sequence[0]) | (sizes[receiver] == 0), 0, jnp.maximum(slack, 0))
    passed = jax.random.randint(jax.random.fold_in(own, 4), (number_of // 2,), 0, 1 << 20) % (slack + 1)
    sizes = sizes.at[donor].add(-passed).at[receiver].add(passed)
    members = jnp.searchsorted(jnp.cumsum(sizes), jnp.arange(rows * top), side="right").astype(jnp.int32)
    table = members.reshape(top, rows).T
    table = table[jax.random.permutation(jax.random.fold_in(own, 1), rows)]
    turn = jax.random.randint(jax.random.fold_in(own, 2), (rows, 1), 0, top)
    return jnp.take_along_axis(table, (jnp.arange(top)[None, :] + turn) % top, axis=1)


def load_shares(count, total, most, slope, full):
    weights = [(1 << 20) // math.isqrt(grade ** slope) + 1 for grade in range(1, count + 1)]
    largest = most if full else min(most, max(-(-total // count), total * weights[0] // sum(weights)))
    least = 1 if total - largest >= count - 1 else 0
    given, spare = [largest] + [least] * (count - 1), total - largest - least * (count - 1)
    while spare > 0:
        candidates = [i for i in range(1, count) if given[i] < largest] or [i for i in range(1, count) if given[i] < most]
        pool, remaining = sum([weights[i] for i in candidates]), spare
        for i in candidates:
            addition = min(most - given[i], max(1, remaining * weights[i] // pool), spare)
            given[i] = given[i] + addition
            spare = spare - addition
    return np.array(given)


def normal_values(stream_key, shape, deviation, reach, cuts=(), held_as=jnp.bfloat16):
    level = block_scale(stream_key, shape, cuts, -0.22, 0.18) if cuts else 1.0
    entries = jax.random.normal(stream_key, shape, jnp.float32) * deviation * level
    return jnp.minimum(jnp.maximum(entries, -reach), reach).astype(held_as)


def setup_inputs(seed: int = 0, part: int = 0) -> dict:
    keys = jax.random.split(jax.random.key(seed), 16)
    part_keys = jax.random.split(jax.random.fold_in(keys[15], part), 16)
    residual = normal_values(part_keys[0], (TOKENS, D), 1.0, 6.0, ((0, 16),))
    queries = draw_queries(jax.random.fold_in(jax.random.fold_in(keys[15], part), 71), part)
    tree_row_keys = normal_values(part_keys[2], (REQUEST_COUNT, TREE_ROWS, KEY_HEADS * HEAD_SIZE), 1.0, 6.0, ((0, 8), (2, 2)))
    tree_row_values = normal_values(part_keys[3], (REQUEST_COUNT, TREE_ROWS, KEY_HEADS * HEAD_SIZE), 1.0, 6.0, ((0, 8), (2, 2)))
    cache_keys = draw_cache_keys(jax.random.fold_in(jax.random.fold_in(keys[15], part), 71), part)
    stored_values = normal_values(part_keys[5], (REQUEST_COUNT, CACHE_SLOTS, KEY_HEADS * HEAD_SIZE), 1.0, 6.0, ((0, 8), (2, 2)))
    cache_lengths = draw_cache_lengths(jax.random.fold_in(jax.random.fold_in(keys[15], part), 71), part)
    tree_sizes = draw_tree_sizes(jax.random.fold_in(jax.random.fold_in(keys[15], part), 71), part)
    tree_mask = draw_tree_mask(jax.random.fold_in(jax.random.fold_in(keys[15], part), 71), part)
    routes_keys = jax.random.split(jax.random.fold_in(part_keys[9], 1), TOKENS // ROWS_DEV)
    routes_turns = jax.random.permutation(jax.random.fold_in(part_keys[9], 3), TOKENS // ROWS_DEV)
    routes = jax.vmap(lambda own, number: deal_out(jax.random.fold_in(part_keys[9], 2), own, number, ROWS_DEV, EXPERTS, 2, CAP, 2))(routes_keys, routes_turns).reshape((TOKENS, 2))
    norm_gain = jnp.clip(1.0 + 0.18 * jax.random.normal(keys[10], (D,), jnp.float32), 0.099609375, 1.8984375).astype(jnp.bfloat16)
    router = normal_values(keys[11], (D, EXPERTS), D ** -0.5, 0.109375)
    gate_weight = normal_values(keys[12], (D, EXPERTS * FF), D ** -0.5, 0.109375, ((0, 2), (1, 8)))
    up_weight = normal_values(keys[13], (D, EXPERTS * FF), D ** -0.5, 0.109375, ((0, 2), (1, 8)))
    down_weight = normal_values(keys[14], (EXPERTS * FF, D), FF ** -0.5, 0.0625, ((0, 8), (1, 2)))
    return dict(residual=residual, queries=queries, tree_row_keys=tree_row_keys, tree_row_values=tree_row_values, cache_keys=cache_keys, stored_values=stored_values, cache_lengths=cache_lengths, tree_sizes=tree_sizes, tree_mask=tree_mask, routes=routes, norm_gain=norm_gain, router=router, gate_weight=gate_weight, up_weight=up_weight, down_weight=down_weight)


def attend_request(query_rows, tree_key_rows, tree_value_rows, cache_key_rows, cache_value_rows, length, tree_size, mask_r):
    heads_per_group = QUERY_HEADS // KEY_HEADS
    query_head_count = query_rows.astype(jnp.float32).reshape(TREE_ROWS, KEY_HEADS, heads_per_group, HEAD_SIZE)
    cache_key_block = cache_key_rows.astype(jnp.float32).reshape(CACHE_SLOTS, KEY_HEADS, HEAD_SIZE)
    cache_value_block = cache_value_rows.astype(jnp.float32).reshape(CACHE_SLOTS, KEY_HEADS, HEAD_SIZE)
    tree_key_block = tree_key_rows.astype(jnp.float32).reshape(TREE_ROWS, KEY_HEADS, HEAD_SIZE)
    tree_value_block = tree_value_rows.astype(jnp.float32).reshape(TREE_ROWS, KEY_HEADS, HEAD_SIZE)
    scale = 1.0 / math.sqrt(HEAD_SIZE)
    cache_scores = jnp.einsum('tgqd,cgd->gqtc', query_head_count, cache_key_block) * scale
    tree_scores = jnp.einsum('tgqd,ugd->gqtu', query_head_count, tree_key_block) * scale
    cache_live = jnp.arange(CACHE_SLOTS, dtype=jnp.int32) < length
    tree_live = (mask_r > 0) & (jnp.arange(TREE_ROWS, dtype=jnp.int32)[None, :] < tree_size)
    cache_scores = jnp.where(cache_live[None, None, None, :], cache_scores, -1e+30)
    tree_scores = jnp.where(tree_live[None, None], tree_scores, -1e+30)
    highest = jnp.maximum(cache_scores.max(-1), tree_scores.max(-1))
    cache_exp = jnp.exp(cache_scores - highest[..., None])
    tree_exp = jnp.exp(tree_scores - highest[..., None])
    summed = cache_exp.sum(-1) + tree_exp.sum(-1)
    cache_prob = (cache_exp / summed[..., None]).astype(jnp.bfloat16).astype(jnp.float32)
    tree_prob = (tree_exp / summed[..., None]).astype(jnp.bfloat16).astype(jnp.float32)
    output = jnp.einsum('gqtc,cgd->tgqd', cache_prob, cache_value_block) + jnp.einsum('gqtu,ugd->tgqd', tree_prob, tree_value_block)
    return output.reshape(TREE_ROWS, QUERY_HEADS * HEAD_SIZE).astype(jnp.bfloat16)

def place_rows(route_block):
    flat_routes = route_block.reshape(-1)
    onehot = (flat_routes[:, None] == jnp.arange(EXPERTS, dtype=jnp.int32)[None, :]).astype(jnp.int32)
    before = jnp.cumsum(onehot, axis=0) - onehot
    position = lax.optimization_barrier(jnp.sum(before * onehot, axis=1))
    return (flat_routes * CAP + position).astype(jnp.int32)

def reference(residual, queries, tree_row_keys, tree_row_values, cache_keys, stored_values, cache_lengths, tree_sizes, tree_mask, routes, norm_gain, router, gate_weight, up_weight, down_weight):
    attended = lax.map(lambda items: attend_request(*items), (queries, tree_row_keys, tree_row_values, cache_keys, stored_values, cache_lengths, tree_sizes, tree_mask))
    attended = attended.reshape(TOKENS, D)
    stream = residual.astype(jnp.float32) + attended.astype(jnp.float32)
    normed = (stream * lax.rsqrt(lax.optimization_barrier(jnp.mean(stream * stream, axis=-1, keepdims=True)) + 1e-05) * norm_gain.astype(jnp.float32)).astype(jnp.bfloat16)
    blocks_count = TOKENS // ROWS_DEV
    normed_blocks = normed.reshape(blocks_count, ROWS_DEV, D)
    targets = jax.vmap(place_rows)(routes.reshape(blocks_count, ROWS_DEV, 2))
    picker = (jnp.arange(EXPERTS * CAP, dtype=jnp.int32)[None, :, None] == targets[:, None, :]).astype(jnp.float32)
    repeated = jnp.repeat(normed_blocks, 2, axis=1).astype(jnp.float32)
    inputs = jnp.einsum('bsr,brd->bsd', picker, repeated).astype(jnp.bfloat16)
    shard_count = N_REQ // EXPERTS * N_HID
    shard_width = FF // shard_count

    def one_expert(expert):
        expert_rows = lax.dynamic_slice_in_dim(inputs, expert * CAP, CAP, 1).reshape(blocks_count * CAP, D)

        def shard_step(carried, shard):
            column = (expert * FF + shard * shard_width).astype(jnp.int32)
            gate = jnp.dot(expert_rows, lax.dynamic_slice_in_dim(gate_weight, column, shard_width, 1), preferred_element_type=jnp.float32)
            up_part = jnp.dot(expert_rows, lax.dynamic_slice_in_dim(up_weight, column, shard_width, 1), preferred_element_type=jnp.float32)
            hidden = (jax.nn.silu(gate) * up_part).astype(jnp.bfloat16)
            partial_out = jnp.dot(hidden, lax.dynamic_slice_in_dim(down_weight, column, shard_width, 0), preferred_element_type=jnp.float32).astype(jnp.bfloat16)
            return (carried + partial_out.astype(jnp.float32), None)
        start = jnp.zeros((blocks_count * CAP, D), jnp.float32)
        summed_out, unused = lax.scan(shard_step, start, jnp.arange(shard_count, dtype=jnp.int32))
        return summed_out.reshape(blocks_count, CAP, D)
    outputs = lax.map(one_expert, jnp.arange(EXPERTS, dtype=jnp.int32))
    outputs = jnp.transpose(outputs, (1, 0, 2, 3)).reshape(blocks_count, EXPERTS * CAP, D)
    picked = jnp.take_along_axis(outputs, targets[:, :, None], axis=1).reshape(TOKENS, 2, D)
    logits = jnp.dot(normed, router, preferred_element_type=jnp.float32)
    chosen = jnp.take_along_axis(logits, routes, axis=1)
    gates = jax.nn.softmax(chosen, axis=-1)
    mixture = lax.optimization_barrier(jnp.sum(gates[:, :, None] * picked, axis=1))
    return (mixture.astype(jnp.bfloat16), (stream + mixture).astype(jnp.bfloat16))
```

```python
import math

import jax
import jax.numpy as jnp
from jax import lax
from jax.experimental import pallas as pl
from jax.experimental.pallas import tpu as pltpu
from jax.sharding import PartitionSpec as P

HEAD_SIZE = 128
EXPERTS = 4


def attend_request(
    query_rows,
    tree_key_rows,
    tree_value_rows,
    cache_key_rows,
    cache_value_rows,
    length,
    tree_size,
    mask_r,
):
    tree_len = query_rows.shape[0]
    cache_len = cache_key_rows.shape[0]
    kv_heads = cache_key_rows.shape[1] // HEAD_SIZE
    query_count = query_rows.shape[1] // HEAD_SIZE
    heads_per_group = query_count // kv_heads
    query_head_count = query_rows.reshape(tree_len, kv_heads, heads_per_group, HEAD_SIZE)
    cache_key_block = cache_key_rows.reshape(cache_len, kv_heads, HEAD_SIZE)
    cache_value_block = cache_value_rows.reshape(cache_len, kv_heads, HEAD_SIZE)
    tree_key_block = tree_key_rows.reshape(tree_len, kv_heads, HEAD_SIZE)
    tree_value_block = tree_value_rows.reshape(tree_len, kv_heads, HEAD_SIZE)
    scale = 1.0 / math.sqrt(HEAD_SIZE)
    cache_scores = (
        jnp.einsum(
            "tgqd,cgd->gqtc", query_head_count, cache_key_block, preferred_element_type=jnp.float32
        )
        * scale
    )
    tree_scores = (
        jnp.einsum(
            "tgqd,ugd->gqtu", query_head_count, tree_key_block, preferred_element_type=jnp.float32
        )
        * scale
    )
    cache_live = jnp.arange(cache_len, dtype=jnp.int32) < length
    tree_live = (mask_r > 0) & (jnp.arange(tree_len, dtype=jnp.int32)[None, :] < tree_size)
    cache_scores = jnp.where(cache_live[None, None, None, :], cache_scores, -1e30)
    tree_scores = jnp.where(tree_live[None, None], tree_scores, -1e30)
    highest = jnp.maximum(cache_scores.max(-1), tree_scores.max(-1))
    cache_exp = jnp.exp(cache_scores - highest[..., None])
    tree_exp = jnp.exp(tree_scores - highest[..., None])
    summed = cache_exp.sum(-1) + tree_exp.sum(-1)
    cache_prob = (cache_exp / summed[..., None]).astype(jnp.bfloat16)
    tree_prob = (tree_exp / summed[..., None]).astype(jnp.bfloat16)
    output = jnp.einsum(
        "gqtc,cgd->tgqd", cache_prob, cache_value_block, preferred_element_type=jnp.float32
    )
    output = output + jnp.einsum(
        "gqtu,ugd->tgqd", tree_prob, tree_value_block, preferred_element_type=jnp.float32
    )
    return output.reshape(tree_len, query_count * HEAD_SIZE).astype(jnp.bfloat16)


def place_rows(route_block, capacity):
    flat_routes = route_block.reshape(-1)
    onehot = (flat_routes[:, None] == jnp.arange(EXPERTS, dtype=jnp.int32)[None, :]).astype(
        jnp.int32
    )
    before = jnp.cumsum(onehot, axis=0) - onehot
    position = jnp.sum(before * onehot, axis=1)
    return flat_routes * capacity + position


def local(
    residual,
    queries,
    tree_row_keys,
    tree_row_values,
    cache_keys,
    stored_values,
    cache_lengths,
    tree_sizes,
    tree_mask,
    routes,
    norm_gain,
    router,
    gate_weight,
    up_weight,
    down_weight,
):
    attended = jax.vmap(attend_request)(
        queries,
        tree_row_keys,
        tree_row_values,
        cache_keys,
        stored_values,
        cache_lengths,
        tree_sizes,
        tree_mask,
    )
    head_rows = attended.reshape(-1, attended.shape[-1])
    own_rows = lax.all_to_all(head_rows, "kv", split_axis=0, concat_axis=1, tiled=True)
    stream = residual.astype(jnp.float32) + own_rows.astype(jnp.float32)
    normed = (
        stream
        * lax.rsqrt(jnp.mean(stream * stream, axis=-1, keepdims=True) + 1e-05)
        * norm_gain.astype(jnp.float32)
    ).astype(jnp.bfloat16)
    row_count = normed.shape[0]
    width = normed.shape[1]
    capacity = row_count * 2 // EXPERTS + max(1, row_count // 8)
    targets = place_rows(routes, capacity)
    picker = (jnp.arange(EXPERTS * capacity, dtype=jnp.int32)[:, None] == targets[None, :]).astype(
        jnp.bfloat16
    )
    blocks = jnp.dot(
        picker, jnp.repeat(normed, 2, axis=0), preferred_element_type=jnp.float32
    ).astype(jnp.bfloat16)
    gate_full, up_full, down_full = (
        lax.all_gather(gate_weight, "kv", axis=0, tiled=True),
        lax.all_gather(up_weight, "kv", axis=0, tiled=True),
        lax.all_gather(down_weight, "kv", axis=1, tiled=True),
    )
    req_count = lax.axis_size("req")
    group_size = req_count // EXPERTS
    outgoing = jnp.repeat(blocks.reshape(EXPERTS, capacity, width), group_size, axis=0)
    arrived = lax.all_to_all(outgoing, "req", split_axis=0, concat_axis=0, tiled=True)
    inputs = lax.all_gather(arrived.reshape(-1, width), "hid", axis=0, tiled=True)
    gate = jnp.dot(inputs, gate_full, preferred_element_type=jnp.float32)
    up_part = jnp.dot(inputs, up_full, preferred_element_type=jnp.float32)
    hidden = (jax.nn.silu(gate) * up_part).astype(jnp.bfloat16)
    partial_out = jnp.dot(hidden, down_full, preferred_element_type=jnp.float32)
    reduced = lax.psum_scatter(
        partial_out.astype(jnp.bfloat16), "hid", scatter_dimension=0, tiled=True
    ).astype(jnp.float32)
    returned = lax.all_to_all(
        reduced.reshape(req_count, capacity, width).astype(jnp.bfloat16),
        "req",
        split_axis=0,
        concat_axis=0,
        tiled=True,
    ).astype(jnp.float32)
    expert_sums = (
        returned.reshape(EXPERTS, group_size, capacity, width)
        .sum(axis=1)
        .reshape(EXPERTS * capacity, width)
    )
    picked = expert_sums[targets].reshape(row_count, 2, width)
    logits = jnp.dot(normed, router, preferred_element_type=jnp.float32)
    chosen = jnp.take_along_axis(logits, routes, axis=1)
    gates = jax.nn.softmax(chosen, axis=-1)
    mixture = jnp.sum(gates[:, :, None] * picked, axis=1)
    return (mixture.astype(jnp.bfloat16), (stream + mixture).astype(jnp.bfloat16))


WAYS = 4
OUT_TILES = 3
MESH = pl.DeviceIdType.MESH


def layer_kernel(
    len_ref, tsz_ref, res_ref, q_ref, tk_ref, tv_ref, mask_ref, routes_ref, gain_ref, router_ref,
    ck_hbm, cv_hbm, wg_hbm, wu_hbm, wd_hbm,
    mix_ref, hid_ref,
    ck, cv, wg, wu, wd,
    xs, xr, sq_s, sq_r, lg_s, lg_r, gates_ref, stream_ref, rows,
    ps, pr, hidden, acc_ref, own_ref, half_s, half_r, summed, back, mixf, hidf, fin_s, fin_r,
    kv_sem, wg_sem, wu_sem, wd_sem, tiny_s, tiny_r, row_zs, row_xs, row_r,
    ps_s, ps_r, h_s, h_r, half_ss, half_rs, back_s, back_r,
):
    req, hid, kv = lax.axis_index("req"), lax.axis_index("hid"), lax.axis_index("kv")
    n_req = rows.shape[0] // 2
    t_rows, half = rows.shape[1], rows.shape[2]
    piece = wg.shape[2]
    tile = wd.shape[2]
    o_rows = res_ref.shape[0]
    okv, ohid = 1 - kv, 1 - hid
    bf, f32 = jnp.bfloat16, jnp.float32
    peer_kv, peer_hid = {"kv": okv}, {"hid": ohid}

    def remote(src, dst, ss, rs, dev):
        return pltpu.make_async_remote_copy(
            src_ref=src, dst_ref=dst, send_sem=ss, recv_sem=rs, device_id=dev, device_id_type=MESH
        )

    copy_k = pltpu.make_async_copy(ck_hbm.at[0], ck, kv_sem.at[0])
    copy_v = pltpu.make_async_copy(cv_hbm.at[0], cv, kv_sem.at[1])
    copy_k.start()
    copy_v.start()

    def weight_copy(which, c):
        hbm, ref, sem = ((wg_hbm, wg, wg_sem), (wu_hbm, wu, wu_sem))[which]
        return pltpu.make_async_copy(
            hbm.at[:, pl.ds(pl.multiple_of(c * piece, piece), piece)], ref.at[c], sem.at[c]
        )

    def down_copy(n):
        return pltpu.make_async_copy(wd_hbm.at[:, pl.ds(n * tile, tile)], wd.at[n], wd_sem.at[n])

    for base in (okv, kv):
        for c in range(WAYS):
            weight_copy(0, base * WAYS + c).start()
            weight_copy(1, base * WAYS + c).start()
    for n in range(OUT_TILES):
        down_copy(n).start()

    barrier = pltpu.get_barrier_semaphore()
    others = [lax.rem(req + d, n_req) for d in range(1, n_req)]
    for dev in [peer_kv, peer_hid] + [{"req": z} for z in others]:
        pl.semaphore_signal(barrier, inc=1, device_id=dev, device_id_type=MESH)
    pl.semaphore_wait(barrier, 2 + len(others))

    lane = lax.broadcasted_iota(jnp.int32, (o_rows, 128), 1)
    routes = routes_ref[...].astype(f32)
    route_lanes = jnp.where(lane == 0, routes[:, 0:1], jnp.where(lane == 1, routes[:, 1:2], 0.0))
    xs[:, :half] = res_ref[:, pl.ds(pl.multiple_of(okv * half, half), half)].astype(f32)
    xs[:, half:] = route_lanes
    swap = remote(xs, xr.at[kv], tiny_s.at[0], tiny_r.at[0], peer_kv)
    swap.start()
    xr[kv, :, :half] = res_ref[:, pl.ds(pl.multiple_of(kv * half, half), half)].astype(f32)
    xr[kv, :, half:] = route_lanes

    scale = 1.0 / math.sqrt(HEAD_SIZE)
    groups = ck.shape[1] // HEAD_SIZE
    per = half // HEAD_SIZE // groups
    length, tsz = len_ref[0], tsz_ref[0]
    mask = mask_ref[0]
    mask = jnp.concatenate([mask] * per, axis=0)
    tree_live = (mask > 0) & (lax.broadcasted_iota(jnp.int32, mask.shape, 1) < tsz)
    slots = ck.shape[0]
    live = lax.broadcasted_iota(jnp.int32, (1, slots), 1) < length
    nt = (((1,), (1,)), ((), ()))
    copy_k.wait()
    heads = []
    scores = []
    for g in range(groups):
        cols = slice(g * HEAD_SIZE, (g + 1) * HEAD_SIZE)
        q = jnp.concatenate(
            [q_ref[0, :, (g * per + j) * HEAD_SIZE : (g * per + j + 1) * HEAD_SIZE] for j in range(per)],
            axis=0,
        )
        s = lax.dot_general(q, ck[:, cols], nt, preferred_element_type=f32) * scale
        t = lax.dot_general(q, tk_ref[0, :, cols], nt, preferred_element_type=f32) * scale
        scores.append((jnp.where(live, s, -1e30), jnp.where(tree_live, t, -1e30)))
    copy_v.wait()
    for g in range(groups):
        cols = slice(g * HEAD_SIZE, (g + 1) * HEAD_SIZE)
        s, t = scores[g]
        top = jnp.maximum(s.max(-1, keepdims=True), t.max(-1, keepdims=True))
        s, t = jnp.exp(s - top), jnp.exp(t - top)
        inv = 1.0 / (s.sum(-1, keepdims=True) + t.sum(-1, keepdims=True))
        o = jnp.dot((s * inv).astype(bf), cv[:, cols], preferred_element_type=f32)
        o = o + jnp.dot((t * inv).astype(bf), tv_ref[0, :, cols], preferred_element_type=f32)
        o = o.astype(bf).astype(f32)
        heads += [o[j * t_rows : (j + 1) * t_rows] for j in range(per)]
    attn = jnp.concatenate(heads, axis=1)

    remote(xs, xr.at[okv], tiny_s.at[0], tiny_r.at[0], peer_kv).wait_recv()
    both = xr[...].reshape(t_rows, half + 128)
    stream = both[:, :half] + attn
    stream_ref[...] = stream
    sq_s[...] = jnp.broadcast_to(jnp.sum(stream * stream, axis=-1, keepdims=True), sq_s.shape)
    swap_sq = remote(sq_s, sq_r, tiny_s.at[1], tiny_r.at[1], peer_kv)
    swap_sq.start()
    gained = gain_ref[:, pl.ds(pl.multiple_of(kv * half, half), half)].astype(f32)
    swap_sq.wait_recv()
    mean = (sq_s[:, 0:1] + sq_r[:, 0:1]) * (1.0 / (2 * half))
    normed = (stream * lax.rsqrt(mean + 1e-05) * gained).astype(bf)

    me = hid * n_req + req
    rows[me] = normed
    sends = []
    for d, z in enumerate(others):
        sends.append(remote(rows.at[me], rows.at[me], row_zs.at[d], row_r.at[me], {"req": z}))
    sends.append(remote(rows.at[me], rows.at[me], row_xs.at[0], row_r.at[me], peer_hid))
    for copy in sends:
        copy.start()

    normed = normed.astype(f32)
    router = router_ref[:, pl.ds(pl.multiple_of(kv * half, half), half)].astype(f32)
    lanes = lax.broadcasted_iota(jnp.int32, (t_rows, 128), 1)
    part = jnp.zeros((t_rows, 128), f32)
    for e in range(EXPERTS):
        one = jnp.sum(normed * router[e : e + 1, :], axis=-1, keepdims=True)
        part = jnp.where(lanes == e, one, part)
    lg_s[...] = part
    swap_lg = remote(lg_s, lg_r, tiny_s.at[2], tiny_r.at[2], peer_kv)
    swap_lg.start()

    def wait_rows(slot):
        remote(rows.at[slot], rows.at[slot], row_xs.at[0], row_r.at[slot], peer_hid).wait_recv()

    for d, z in enumerate(others):
        slot = hid * n_req + z
        wait_rows(slot)
        copy = remote(rows.at[slot], rows.at[slot], row_xs.at[d + 1], row_r.at[slot], peer_hid)
        copy.start()
        sends.append(copy)

    swap_lg.wait_recv()
    logits = lg_s[...] + lg_r[...]
    lane_f = lanes.astype(f32)
    first, second = both[:, half : half + 1], both[:, half + 1 : half + 2]
    is_first, is_second = lane_f == first, lane_f == second
    a = jnp.sum(jnp.where(is_first, logits, 0.0), axis=-1, keepdims=True)
    b = jnp.sum(jnp.where(is_second, logits, 0.0), axis=-1, keepdims=True)
    ab = jnp.maximum(a, b)
    ea, eb = jnp.exp(a - ab), jnp.exp(b - ab)
    gates_ref[...] = jnp.where(is_first, ea / (ea + eb), jnp.where(is_second, eb / (ea + eb), 0.0))

    for z in range(n_req):
        wait_rows(ohid * n_req + lax.rem(req + z, n_req))

    count = 2 * n_req * t_rows

    def both_dots(c):
        weight_copy(0, c).wait()
        weight_copy(1, c).wait()
        x = rows[...].reshape(count, half)
        return (
            jnp.dot(x, wg[c], preferred_element_type=f32),
            jnp.dot(x, wu[c], preferred_element_type=f32),
        )

    def pair_copy(c):
        return remote(ps.at[c], pr.at[c], ps_s.at[c], ps_r.at[c], peer_kv)

    def hidden_copy(which, c):
        view = hidden.at[which, :, pl.ds(pl.multiple_of(c * piece, piece), piece)]
        return remote(view, view, h_s.at[c], h_r.at[c], peer_kv)

    def partner_step(c, _):
        gate, up = both_dots(okv * WAYS + c)
        ps[c, 0] = gate.astype(bf)
        ps[c, 1] = up.astype(bf)
        pair_copy(c).start()
        return 0

    lax.fori_loop(0, WAYS, partner_step, 0)

    def own_step(c, _):
        gate, up = both_dots(kv * WAYS + c)
        pair_copy(c).wait_recv()
        gate = gate + pr[c, 0].astype(f32)
        up = up + pr[c, 1].astype(f32)
        value = (gate / (1.0 + jnp.exp(-gate)) * up).astype(bf)
        hidden[kv, :, pl.ds(pl.multiple_of(c * piece, piece), piece)] = value
        hidden_copy(kv, c).start()
        return 0

    lax.fori_loop(0, WAYS, own_step, 0)

    span = WAYS * piece

    def down_dot(which, n):
        return jnp.dot(
            hidden[which],
            wd[n, pl.ds(pl.multiple_of(which * span, span), span), :],
            preferred_element_type=f32,
        )

    def half_copy(n):
        return remote(half_s.at[n], half_r.at[n], half_ss.at[n], half_rs.at[n], peer_hid)

    def back_copy(n, d, z):
        return remote(
            summed.at[n, z], back.at[n, req], back_s.at[n, d], back_r.at[n, req], {"req": z}
        )

    def forward(n):
        half_copy(n).wait_recv()
        total = (own_ref[n] + half_r[n].astype(f32)).astype(bf)
        summed[n] = total.reshape(n_req, t_rows, tile)
        for d, z in enumerate(others):
            back_copy(n, d, z).start()
        back[n, req] = summed[n, req]

    def down_step(n, _):
        down_copy(n).wait()
        acc_ref[...] = down_dot(kv, n).reshape(acc_ref.shape)

        @pl.when(n == 0)
        def _():
            for c in range(WAYS):
                hidden_copy(okv, c).wait_recv()

        acc_ref[...] += down_dot(okv, n).reshape(acc_ref.shape)
        half_s[n] = acc_ref[ohid].astype(bf)
        half_copy(n).start()
        own_ref[n] = acc_ref[hid]

        @pl.when(n > 0)
        def _():
            forward(n - 1)

        return 0

    lax.fori_loop(0, OUT_TILES, down_step, 0)
    forward(OUT_TILES - 1)

    gates = gates_ref[...]
    for n in range(OUT_TILES):
        for z in others:
            remote(
                summed.at[n, z], back.at[n, z], back_s.at[n, 0], back_r.at[n, z], {"req": z}
            ).wait_recv()
        mix = jnp.zeros((t_rows, tile), f32)
        for e in range(EXPERTS):
            mix = mix + gates[:, e : e + 1] * back[n, e].astype(f32)
        cols = slice(n * tile, (n + 1) * tile)
        mixf[:, :, cols] = mix.reshape(2, o_rows, tile)
        hidf[:, :, cols] = (stream_ref[:, cols] + mix).reshape(2, o_rows, tile)

    fin_s[...] = jnp.concatenate([mixf[okv], hidf[okv]], axis=0).astype(bf)
    last = remote(fin_s, fin_r, tiny_s.at[3], tiny_r.at[3], peer_kv)
    last.start()
    mine = pl.ds(pl.multiple_of(kv * half, half), half)
    mix_ref[:, mine] = mixf[kv].astype(bf)
    hid_ref[:, mine] = hidf[kv].astype(bf)
    last.wait_recv()
    got = fin_r[...].astype(f32)
    theirs = pl.ds(pl.multiple_of(okv * half, half), half)
    mix_ref[:, theirs] = got[:o_rows].astype(bf)
    hid_ref[:, theirs] = got[o_rows:].astype(bf)

    for copy in [swap, swap_sq, swap_lg, last] + sends:
        copy.wait_send()
    for c in range(WAYS):
        pair_copy(c).wait_send()
        hidden_copy(kv, c).wait_send()
    for n in range(OUT_TILES):
        half_copy(n).wait_send()
        for d, z in enumerate(others):
            back_copy(n, d, z).wait_send()


def local_kernel(
    residual, queries, tree_row_keys, tree_row_values, cache_keys, stored_values, cache_lengths,
    tree_sizes, tree_mask, routes, norm_gain, router, gate_weight, up_weight, down_weight,
):
    bf, f32 = jnp.bfloat16, jnp.float32
    n_req = lax.axis_size("req")
    o_rows, width = residual.shape
    half = width // 2
    t_rows = queries.shape[1]
    slots, kv_cols = cache_keys.shape[1:]
    units = gate_weight.shape[1]
    piece = units // 2 // WAYS
    tile = half // OUT_TILES
    count = 2 * n_req * t_rows
    side = n_req * t_rows
    vm = pl.BlockSpec(memory_space=pltpu.VMEM)
    sm = pl.BlockSpec(memory_space=pltpu.SMEM)
    hb = pl.BlockSpec(memory_space=pl.ANY)
    dma = pltpu.SemaphoreType.DMA
    scratch = [
        pltpu.VMEM((slots, kv_cols), bf),
        pltpu.VMEM((slots, kv_cols), bf),
        pltpu.VMEM((2 * WAYS, half, piece), bf),
        pltpu.VMEM((2 * WAYS, half, piece), bf),
        pltpu.VMEM((OUT_TILES, units, tile), bf),
        pltpu.VMEM((o_rows, half + 128), f32),
        pltpu.VMEM((2, o_rows, half + 128), f32),
        pltpu.VMEM((t_rows, 128), f32),
        pltpu.VMEM((t_rows, 128), f32),
        pltpu.VMEM((t_rows, 128), f32),
        pltpu.VMEM((t_rows, 128), f32),
        pltpu.VMEM((t_rows, 128), f32),
        pltpu.VMEM((t_rows, half), f32),
        pltpu.VMEM((2 * n_req, t_rows, half), bf),
        pltpu.VMEM((WAYS, 2, count, piece), bf),
        pltpu.VMEM((WAYS, 2, count, piece), bf),
        pltpu.VMEM((2, count, units // 2), bf),
        pltpu.VMEM((2, side, tile), f32),
        pltpu.VMEM((OUT_TILES, side, tile), f32),
        pltpu.VMEM((OUT_TILES, side, tile), bf),
        pltpu.VMEM((OUT_TILES, side, tile), bf),
        pltpu.VMEM((OUT_TILES, n_req, t_rows, tile), bf),
        pltpu.VMEM((OUT_TILES, n_req, t_rows, tile), bf),
        pltpu.VMEM((2, o_rows, half), f32),
        pltpu.VMEM((2, o_rows, half), f32),
        pltpu.VMEM((t_rows, half), bf),
        pltpu.VMEM((t_rows, half), bf),
        dma((2,)), dma((2 * WAYS,)), dma((2 * WAYS,)), dma((OUT_TILES,)),
        dma((4,)), dma((4,)),
        dma((n_req - 1,)), dma((n_req,)), dma((2 * n_req,)),
        dma((WAYS,)), dma((WAYS,)), dma((WAYS,)), dma((WAYS,)),
        dma((OUT_TILES,)), dma((OUT_TILES,)),
        dma((OUT_TILES, n_req - 1)), dma((OUT_TILES, n_req)),
    ]
    return pl.pallas_call(
        layer_kernel,
        out_shape=(jax.ShapeDtypeStruct(residual.shape, bf),) * 2,
        in_specs=[sm, sm] + [vm] * 8 + [hb] * 5,
        out_specs=(vm, vm),
        scratch_shapes=scratch,
        compiler_params=pltpu.CompilerParams(
            collective_id=0, has_side_effects=True, vmem_limit_bytes=58 * 1024 * 1024
        ),
        cost_estimate=pl.CostEstimate(
            flops=6 * count * half * units, bytes_accessed=6 * half * units, transcendentals=0
        ),
    )(
        cache_lengths, tree_sizes, residual, queries, tree_row_keys, tree_row_values, tree_mask,
        routes, norm_gain.reshape(1, -1), router.T,
        cache_keys, stored_values, gate_weight, up_weight, down_weight,
    )


def solution(mesh):
    placed = (
        P(("grp", "req", "hid", "kv"), None),
        P(("grp", "req", "hid"), None, "kv"),
        P(("grp", "req", "hid"), None, "kv"),
        P(("grp", "req", "hid"), None, "kv"),
        P(("grp", "req", "hid"), None, "kv"),
        P(("grp", "req", "hid"), None, "kv"),
        P(("grp", "req", "hid")),
        P(("grp", "req", "hid")),
        P(("grp", "req", "hid"), None, None),
        P(("grp", "req", "hid", "kv"), None),
        P(),
        P(),
        P("kv", ("req", "hid")),
        P("kv", ("req", "hid")),
        P(("req", "hid"), "kv"),
    )
    one_shard_per_expert = mesh.shape["req"] == EXPERTS and mesh.shape["hid"] == 2
    return jax.shard_map(
        local_kernel if one_shard_per_expert and mesh.shape["kv"] == 2 else local,
        mesh=mesh,
        in_specs=placed,
        out_specs=(P(("grp", "req", "hid", "kv"), None), P(("grp", "req", "hid", "kv"), None)),
        check_vma=False,
    )
```

```python
import math

import jax
import jax.numpy as jnp
from jax import lax
from jax.experimental import pallas as pl
from jax.experimental.pallas import tpu as pltpu
from jax.sharding import PartitionSpec as P

HEAD_SIZE = 128
EXPERTS = 4


def attend_request(
    query_rows,
    tree_key_rows,
    tree_value_rows,
    cache_key_rows,
    cache_value_rows,
    length,
    tree_size,
    mask_r,
):
    tree_len = query_rows.shape[0]
    cache_len = cache_key_rows.shape[0]
    kv_heads = cache_key_rows.shape[1] // HEAD_SIZE
    query_count = query_rows.shape[1] // HEAD_SIZE
    heads_per_group = query_count // kv_heads
    query_head_count = query_rows.reshape(tree_len, kv_heads, heads_per_group, HEAD_SIZE)
    cache_key_block = cache_key_rows.reshape(cache_len, kv_heads, HEAD_SIZE)
    cache_value_block = cache_value_rows.reshape(cache_len, kv_heads, HEAD_SIZE)
    tree_key_block = tree_key_rows.reshape(tree_len, kv_heads, HEAD_SIZE)
    tree_value_block = tree_value_rows.reshape(tree_len, kv_heads, HEAD_SIZE)
    scale = 1.0 / math.sqrt(HEAD_SIZE)
    cache_scores = (
        jnp.einsum(
            "tgqd,cgd->gqtc", query_head_count, cache_key_block, preferred_element_type=jnp.float32
        )
        * scale
    )
    tree_scores = (
        jnp.einsum(
            "tgqd,ugd->gqtu", query_head_count, tree_key_block, preferred_element_type=jnp.float32
        )
        * scale
    )
    cache_live = jnp.arange(cache_len, dtype=jnp.int32) < length
    tree_live = (mask_r > 0) & (jnp.arange(tree_len, dtype=jnp.int32)[None, :] < tree_size)
    cache_scores = jnp.where(cache_live[None, None, None, :], cache_scores, -1e30)
    tree_scores = jnp.where(tree_live[None, None], tree_scores, -1e30)
    highest = jnp.maximum(cache_scores.max(-1), tree_scores.max(-1))
    cache_exp = jnp.exp(cache_scores - highest[..., None])
    tree_exp = jnp.exp(tree_scores - highest[..., None])
    summed = cache_exp.sum(-1) + tree_exp.sum(-1)
    cache_prob = (cache_exp / summed[..., None]).astype(jnp.bfloat16)
    tree_prob = (tree_exp / summed[..., None]).astype(jnp.bfloat16)
    output = jnp.einsum(
        "gqtc,cgd->tgqd", cache_prob, cache_value_block, preferred_element_type=jnp.float32
    )
    output = output + jnp.einsum(
        "gqtu,ugd->tgqd", tree_prob, tree_value_block, preferred_element_type=jnp.float32
    )
    return output.reshape(tree_len, query_count * HEAD_SIZE).astype(jnp.bfloat16)


def place_rows(route_block, capacity):
    flat_routes = route_block.reshape(-1)
    onehot = (flat_routes[:, None] == jnp.arange(EXPERTS, dtype=jnp.int32)[None, :]).astype(
        jnp.int32
    )
    before = jnp.cumsum(onehot, axis=0) - onehot
    position = jnp.sum(before * onehot, axis=1)
    return flat_routes * capacity + position


def local(
    residual,
    queries,
    tree_row_keys,
    tree_row_values,
    cache_keys,
    stored_values,
    cache_lengths,
    tree_sizes,
    tree_mask,
    routes,
    norm_gain,
    router,
    gate_weight,
    up_weight,
    down_weight,
):
    attended = jax.vmap(attend_request)(
        queries,
        tree_row_keys,
        tree_row_values,
        cache_keys,
        stored_values,
        cache_lengths,
        tree_sizes,
        tree_mask,
    )
    head_rows = attended.reshape(-1, attended.shape[-1])
    own_rows = lax.all_to_all(head_rows, "kv", split_axis=0, concat_axis=1, tiled=True)
    stream = residual.astype(jnp.float32) + own_rows.astype(jnp.float32)
    normed = (
        stream
        * lax.rsqrt(jnp.mean(stream * stream, axis=-1, keepdims=True) + 1e-05)
        * norm_gain.astype(jnp.float32)
    ).astype(jnp.bfloat16)
    row_count = normed.shape[0]
    width = normed.shape[1]
    capacity = row_count * 2 // EXPERTS + max(1, row_count // 8)
    targets = place_rows(routes, capacity)
    picker = (jnp.arange(EXPERTS * capacity, dtype=jnp.int32)[:, None] == targets[None, :]).astype(
        jnp.bfloat16
    )
    blocks = jnp.dot(
        picker, jnp.repeat(normed, 2, axis=0), preferred_element_type=jnp.float32
    ).astype(jnp.bfloat16)
    gate_full, up_full, down_full = (
        lax.all_gather(gate_weight, "kv", axis=0, tiled=True),
        lax.all_gather(up_weight, "kv", axis=0, tiled=True),
        lax.all_gather(down_weight, "kv", axis=1, tiled=True),
    )
    req_count = lax.axis_size("req")
    group_size = req_count // EXPERTS
    outgoing = jnp.repeat(blocks.reshape(EXPERTS, capacity, width), group_size, axis=0)
    arrived = lax.all_to_all(outgoing, "req", split_axis=0, concat_axis=0, tiled=True)
    inputs = lax.all_gather(arrived.reshape(-1, width), "hid", axis=0, tiled=True)
    gate = jnp.dot(inputs, gate_full, preferred_element_type=jnp.float32)
    up_part = jnp.dot(inputs, up_full, preferred_element_type=jnp.float32)
    hidden = (jax.nn.silu(gate) * up_part).astype(jnp.bfloat16)
    partial_out = jnp.dot(hidden, down_full, preferred_element_type=jnp.float32)
    reduced = lax.psum_scatter(
        partial_out.astype(jnp.bfloat16), "hid", scatter_dimension=0, tiled=True
    ).astype(jnp.float32)
    returned = lax.all_to_all(
        reduced.reshape(req_count, capacity, width).astype(jnp.bfloat16),
        "req",
        split_axis=0,
        concat_axis=0,
        tiled=True,
    ).astype(jnp.float32)
    expert_sums = (
        returned.reshape(EXPERTS, group_size, capacity, width)
        .sum(axis=1)
        .reshape(EXPERTS * capacity, width)
    )
    picked = expert_sums[targets].reshape(row_count, 2, width)
    logits = jnp.dot(normed, router, preferred_element_type=jnp.float32)
    chosen = jnp.take_along_axis(logits, routes, axis=1)
    gates = jax.nn.softmax(chosen, axis=-1)
    mixture = jnp.sum(gates[:, :, None] * picked, axis=1)
    return (mixture.astype(jnp.bfloat16), (stream + mixture).astype(jnp.bfloat16))


WAYS = 2
OUT_TILES = 2
MESH = pl.DeviceIdType.MESH
FAR = (1, 3, 2)


def layer_kernel(
    len_ref, tsz_ref, res_ref, q_ref, tk_ref, tv_ref, mask_ref, routes_ref, gain_ref, router_ref,
    ck_hbm, cv_hbm, wg_hbm, wu_hbm, wd_hbm,
    out_ref,
    ck, cv, wg, wu, wd,
    xs, xr, sq_s, sq_r, lg_s, lg_r, gates_ref, stream_ref, rows,
    ps, pr, hidden, acc_ref, own_ref, half_s, half_r, summed, back, mixf, hidf, fin_s, fin_r,
    kv_sem, wg_sem, wu_sem, wd_sem, tiny_s, tiny_r, row_zs, row_xs, row_r,
    ps_s, ps_r, h_s, h_r, half_ss, half_rs, back_s, back_r,
):
    req, hid, kv = lax.axis_index("req"), lax.axis_index("hid"), lax.axis_index("kv")
    n_req = rows.shape[0] // 2
    t_rows, half = rows.shape[1], rows.shape[2]
    piece = wg.shape[2]
    tile = wd.shape[2]
    o_rows = res_ref.shape[0]
    okv, ohid = 1 - kv, 1 - hid
    bf, f32 = jnp.bfloat16, jnp.float32
    peer_kv, peer_hid = {"kv": okv}, {"hid": ohid}

    def remote(src, dst, ss, rs, dev):
        return pltpu.make_async_remote_copy(
            src_ref=src, dst_ref=dst, send_sem=ss, recv_sem=rs, device_id=dev, device_id_type=MESH
        )

    copy_k = pltpu.make_async_copy(ck_hbm.at[0], ck, kv_sem.at[0])
    copy_v = pltpu.make_async_copy(cv_hbm.at[0], cv, kv_sem.at[1])
    copy_k.start()
    copy_v.start()

    def weight_copy(which, c):
        hbm, ref, sem = ((wg_hbm, wg, wg_sem), (wu_hbm, wu, wu_sem))[which]
        return pltpu.make_async_copy(
            hbm.at[:, pl.ds(pl.multiple_of(c * piece, piece), piece)], ref.at[c], sem.at[c]
        )

    def down_copy(n):
        return pltpu.make_async_copy(wd_hbm.at[:, pl.ds(n * tile, tile)], wd.at[n], wd_sem.at[n])


    barrier = pltpu.get_barrier_semaphore()
    others = [lax.rem(req + d, n_req) for d in FAR]
    for dev in [peer_kv, peer_hid] + [{"req": z} for z in others]:
        pl.semaphore_signal(barrier, inc=1, device_id=dev, device_id_type=MESH)

    scale = 1.0 / math.sqrt(HEAD_SIZE)
    groups = ck.shape[1] // HEAD_SIZE
    per = half // HEAD_SIZE // groups
    length, tsz = len_ref[0], tsz_ref[0]
    mask = mask_ref[0]
    mask = jnp.concatenate([mask] * per, axis=0)
    tree_live = (mask > 0) & (lax.broadcasted_iota(jnp.int32, mask.shape, 1) < tsz)
    slots = ck.shape[0]
    live = lax.broadcasted_iota(jnp.int32, (1, slots), 1) < length
    nt = (((1,), (1,)), ((), ()))
    copy_k.wait()
    heads = []
    scores = []
    for g in range(groups):
        cols = slice(g * HEAD_SIZE, (g + 1) * HEAD_SIZE)
        q = jnp.concatenate(
            [q_ref[0, :, (g * per + j) * HEAD_SIZE : (g * per + j + 1) * HEAD_SIZE] for j in range(per)],
            axis=0,
        )
        s = lax.dot_general(q, ck[:, cols], nt, preferred_element_type=f32) * scale
        t = lax.dot_general(q, tk_ref[0, :, cols], nt, preferred_element_type=f32) * scale
        scores.append((jnp.where(live, s, -1e30), jnp.where(tree_live, t, -1e30)))
    pl.semaphore_wait(barrier, 2 + len(others))

    lane = lax.broadcasted_iota(jnp.int32, (o_rows, 128), 1)
    routes = routes_ref[...].astype(f32)
    square = (o_rows, o_rows)
    diagonal = lax.broadcasted_iota(jnp.int32, square, 0) == lax.broadcasted_iota(jnp.int32, square, 1)
    choice = [
        jnp.sum(jnp.where(diagonal, routes[k : k + 1, :], 0.0), axis=1, keepdims=True) for k in range(2)
    ]
    route_lanes = jnp.where(lane == 0, choice[0], jnp.where(lane == 1, choice[1], 0.0))
    xs[:, :half] = res_ref[:, pl.ds(pl.multiple_of(okv * half, half), half)].astype(f32)
    xs[:, half:] = route_lanes
    swap = remote(xs, xr.at[kv], tiny_s.at[0], tiny_r.at[0], peer_kv)
    swap.start()
    xr[kv, :, :half] = res_ref[:, pl.ds(pl.multiple_of(kv * half, half), half)].astype(f32)
    xr[kv, :, half:] = route_lanes

    copy_v.wait()
    for base in (okv, kv):
        for c in range(WAYS):
            weight_copy(0, base * WAYS + c).start()
            weight_copy(1, base * WAYS + c).start()
    for g in range(groups):
        cols = slice(g * HEAD_SIZE, (g + 1) * HEAD_SIZE)
        s, t = scores[g]
        top = jnp.maximum(s.max(-1, keepdims=True), t.max(-1, keepdims=True))
        s, t = jnp.exp(s - top), jnp.exp(t - top)
        inv = 1.0 / (s.sum(-1, keepdims=True) + t.sum(-1, keepdims=True))
        o = jnp.dot((s * inv).astype(bf), cv[:, cols], preferred_element_type=f32)
        o = o + jnp.dot((t * inv).astype(bf), tv_ref[0, :, cols], preferred_element_type=f32)
        o = o.astype(bf).astype(f32)
        heads += [o[j * t_rows : (j + 1) * t_rows] for j in range(per)]
    attn = jnp.concatenate(heads, axis=1)

    remote(xs, xr.at[okv], tiny_s.at[0], tiny_r.at[0], peer_kv).wait_recv()
    both = xr[...].reshape(t_rows, half + 128)
    stream = both[:, :half] + attn
    stream_ref[...] = stream
    sq_s[...] = jnp.broadcast_to(jnp.sum(stream * stream, axis=-1, keepdims=True), sq_s.shape)
    swap_sq = remote(sq_s, sq_r, tiny_s.at[1], tiny_r.at[1], peer_kv)
    swap_sq.start()
    gain = gain_ref[...].astype(f32)
    strips = half // 128
    gain = jnp.where(kv == 0, gain[:strips], gain[strips:])
    gained = jnp.concatenate([gain[j : j + 1] for j in range(strips)], axis=1)
    swap_sq.wait_recv()
    mean = (sq_s[:, 0:1] + sq_r[:, 0:1]) * (1.0 / (2 * half))
    normed = (stream * lax.rsqrt(mean + 1e-05) * gained).astype(bf)

    me = hid * n_req + req
    rows[me] = normed
    sends = []
    for d, z in enumerate(others):
        sends.append(remote(rows.at[me], rows.at[me], row_zs.at[d], row_r.at[me], {"req": z}))
    sends.append(remote(rows.at[me], rows.at[me], row_xs.at[0], row_r.at[me], peer_hid))
    for copy in sends:
        copy.start()

    normed = normed.astype(f32)
    router = router_ref[:, pl.ds(pl.multiple_of(kv * half, half), half)].astype(f32)
    lanes = lax.broadcasted_iota(jnp.int32, (t_rows, 128), 1)
    part = jnp.zeros((t_rows, 128), f32)
    for e in range(EXPERTS):
        one = jnp.sum(normed * router[e : e + 1, :], axis=-1, keepdims=True)
        part = jnp.where(lanes == e, one, part)
    lg_s[...] = part
    swap_lg = remote(lg_s, lg_r, tiny_s.at[2], tiny_r.at[2], peer_kv)
    swap_lg.start()

    def wait_rows(slot):
        remote(rows.at[slot], rows.at[slot], row_xs.at[0], row_r.at[slot], peer_hid).wait_recv()

    for d, z in enumerate(others):
        slot = hid * n_req + z
        wait_rows(slot)
        copy = remote(rows.at[slot], rows.at[slot], row_xs.at[d + 1], row_r.at[slot], peer_hid)
        copy.start()
        sends.append(copy)

    swap_lg.wait_recv()
    logits = lg_s[...] + lg_r[...]
    lane_f = lanes.astype(f32)
    first, second = both[:, half : half + 1], both[:, half + 1 : half + 2]
    is_first, is_second = lane_f == first, lane_f == second
    a = jnp.sum(jnp.where(is_first, logits, 0.0), axis=-1, keepdims=True)
    b = jnp.sum(jnp.where(is_second, logits, 0.0), axis=-1, keepdims=True)
    ab = jnp.maximum(a, b)
    ea, eb = jnp.exp(a - ab), jnp.exp(b - ab)
    gates_ref[...] = jnp.where(is_first, ea / (ea + eb), jnp.where(is_second, eb / (ea + eb), 0.0))

    for z in range(n_req):
        wait_rows(ohid * n_req + lax.rem(req + z, n_req))

    for n in range(OUT_TILES):
        down_copy(n).start()
    count = 2 * n_req * t_rows

    def both_dots(c):
        weight_copy(0, c).wait()
        weight_copy(1, c).wait()
        x = rows[...].reshape(count, half)
        return (
            jnp.dot(x, wg[c], preferred_element_type=f32),
            jnp.dot(x, wu[c], preferred_element_type=f32),
        )

    def pair_copy(c):
        return remote(ps.at[c], pr.at[c], ps_s.at[c], ps_r.at[c], peer_kv)

    def hidden_copy(which, c):
        view = hidden.at[which, :, pl.ds(pl.multiple_of(c * piece, piece), piece)]
        return remote(view, view, h_s.at[c], h_r.at[c], peer_kv)

    def partner_step(c, _):
        gate, up = both_dots(okv * WAYS + c)
        ps[c, 0] = gate.astype(bf)
        ps[c, 1] = up.astype(bf)
        pair_copy(c).start()
        return 0

    lax.fori_loop(0, WAYS, partner_step, 0)

    def own_step(c, _):
        gate, up = both_dots(kv * WAYS + c)
        pair_copy(c).wait_recv()
        gate = gate + pr[c, 0].astype(f32)
        up = up + pr[c, 1].astype(f32)
        value = (gate / (1.0 + jnp.exp(-gate)) * up).astype(bf)
        hidden[kv, :, pl.ds(pl.multiple_of(c * piece, piece), piece)] = value
        hidden_copy(kv, c).start()
        return 0

    lax.fori_loop(0, WAYS, own_step, 0)

    span = WAYS * piece

    def down_dot(which, n):
        return jnp.dot(
            hidden[which],
            wd[n, pl.ds(pl.multiple_of(which * span, span), span), :],
            preferred_element_type=f32,
        )

    def half_copy(n):
        return remote(half_s.at[n], half_r.at[n], half_ss.at[n], half_rs.at[n], peer_hid)

    def back_copy(n, d, z):
        return remote(
            summed.at[n, z], back.at[n, req], back_s.at[n, d], back_r.at[n, req], {"req": z}
        )

    def forward(n):
        half_copy(n).wait_recv()
        total = (own_ref[n] + half_r[n].astype(f32)).astype(bf)
        summed[n] = total.reshape(n_req, t_rows, tile)
        for d, z in enumerate(others):
            back_copy(n, d, z).start()
        back[n, req] = summed[n, req]

    def down_step(n, _):
        down_copy(n).wait()
        acc_ref[...] = down_dot(kv, n).reshape(acc_ref.shape)

        @pl.when(n == 0)
        def _():
            for c in range(WAYS):
                hidden_copy(okv, c).wait_recv()

        acc_ref[...] += down_dot(okv, n).reshape(acc_ref.shape)
        half_s[n] = acc_ref[ohid].astype(bf)
        half_copy(n).start()
        own_ref[n] = acc_ref[hid]

        @pl.when(n > 0)
        def _():
            forward(n - 1)

        return 0

    lax.fori_loop(0, OUT_TILES, down_step, 0)
    forward(OUT_TILES - 1)

    gates = gates_ref[...]
    for n in range(OUT_TILES):
        for z in others:
            remote(
                summed.at[n, z], back.at[n, z], back_s.at[n, 0], back_r.at[n, z], {"req": z}
            ).wait_recv()
        mix = jnp.zeros((t_rows, tile), f32)
        for e in range(EXPERTS):
            mix = mix + gates[:, e : e + 1] * back[n, e].astype(f32)
        cols = slice(n * tile, (n + 1) * tile)
        mixf[:, :, cols] = mix.reshape(2, o_rows, tile)
        hidf[:, :, cols] = (stream_ref[:, cols] + mix).reshape(2, o_rows, tile)

    fin_s[...] = jnp.concatenate([mixf[okv], hidf[okv]], axis=0).astype(bf)
    last = remote(fin_s, fin_r, tiny_s.at[3], tiny_r.at[3], peer_kv)
    last.start()
    mine = pl.ds(pl.multiple_of(kv * half, half), half)
    out_ref[:, mine] = jnp.concatenate([mixf[kv], hidf[kv]], axis=0).astype(bf)
    last.wait_recv()
    theirs = pl.ds(pl.multiple_of(okv * half, half), half)
    out_ref[:, theirs] = fin_r[...]

    for copy in [swap, swap_sq, swap_lg, last] + sends:
        copy.wait_send()
    for c in range(WAYS):
        pair_copy(c).wait_send()
        hidden_copy(kv, c).wait_send()
    for n in range(OUT_TILES):
        half_copy(n).wait_send()
        for d, z in enumerate(others):
            back_copy(n, d, z).wait_send()


def local_kernel(
    residual, queries, tree_row_keys, tree_row_values, cache_keys, stored_values, cache_lengths,
    tree_sizes, tree_mask, routes, norm_gain, router, gate_weight, up_weight, down_weight,
):
    bf, f32 = jnp.bfloat16, jnp.float32
    n_req = lax.axis_size("req")
    o_rows, width = residual.shape
    half = width // 2
    t_rows = queries.shape[1]
    slots, kv_cols = cache_keys.shape[1:]
    units = gate_weight.shape[1]
    piece = units // 2 // WAYS
    tile = half // OUT_TILES
    count = 2 * n_req * t_rows
    side = n_req * t_rows
    vm = pl.BlockSpec(memory_space=pltpu.VMEM)
    sm = pl.BlockSpec(memory_space=pltpu.SMEM)
    hb = pl.BlockSpec(memory_space=pl.ANY)
    dma = pltpu.SemaphoreType.DMA
    scratch = [
        pltpu.VMEM((slots, kv_cols), bf),
        pltpu.VMEM((slots, kv_cols), bf),
        pltpu.VMEM((2 * WAYS, half, piece), bf),
        pltpu.VMEM((2 * WAYS, half, piece), bf),
        pltpu.VMEM((OUT_TILES, units, tile), bf),
        pltpu.VMEM((o_rows, half + 128), f32),
        pltpu.VMEM((2, o_rows, half + 128), f32),
        pltpu.VMEM((t_rows, 128), f32),
        pltpu.VMEM((t_rows, 128), f32),
        pltpu.VMEM((t_rows, 128), f32),
        pltpu.VMEM((t_rows, 128), f32),
        pltpu.VMEM((t_rows, 128), f32),
        pltpu.VMEM((t_rows, half), f32),
        pltpu.VMEM((2 * n_req, t_rows, half), bf),
        pltpu.VMEM((WAYS, 2, count, piece), bf),
        pltpu.VMEM((WAYS, 2, count, piece), bf),
        pltpu.VMEM((2, count, units // 2), bf),
        pltpu.VMEM((2, side, tile), f32),
        pltpu.VMEM((OUT_TILES, side, tile), f32),
        pltpu.VMEM((OUT_TILES, side, tile), bf),
        pltpu.VMEM((OUT_TILES, side, tile), bf),
        pltpu.VMEM((OUT_TILES, n_req, t_rows, tile), bf),
        pltpu.VMEM((OUT_TILES, n_req, t_rows, tile), bf),
        pltpu.VMEM((2, o_rows, half), f32),
        pltpu.VMEM((2, o_rows, half), f32),
        pltpu.VMEM((t_rows, half), bf),
        pltpu.VMEM((t_rows, half), bf),
        dma((2,)), dma((2 * WAYS,)), dma((2 * WAYS,)), dma((OUT_TILES,)),
        dma((4,)), dma((4,)),
        dma((n_req - 1,)), dma((n_req,)), dma((2 * n_req,)),
        dma((WAYS,)), dma((WAYS,)), dma((WAYS,)), dma((WAYS,)),
        dma((OUT_TILES,)), dma((OUT_TILES,)),
        dma((OUT_TILES, n_req - 1)), dma((OUT_TILES, n_req)),
    ]
    both = pl.pallas_call(
        layer_kernel,
        out_shape=jax.ShapeDtypeStruct((2 * o_rows, width), bf),
        in_specs=[sm, sm] + [vm] * 8 + [hb] * 5,
        out_specs=vm,
        scratch_shapes=scratch,
        compiler_params=pltpu.CompilerParams(
            collective_id=0, has_side_effects=True, vmem_limit_bytes=58 * 1024 * 1024
        ),
        cost_estimate=pl.CostEstimate(
            flops=6 * count * half * units, bytes_accessed=6 * half * units, transcendentals=0
        ),
    )(
        cache_lengths, tree_sizes, residual, queries, tree_row_keys, tree_row_values, tree_mask,
        routes.T, norm_gain.reshape(-1, 128), router.T,
        cache_keys, stored_values, gate_weight, up_weight, down_weight,
    )
    return both[:o_rows], both[o_rows:]


def solution(mesh):
    placed = (
        P(("grp", "req", "hid", "kv"), None),
        P(("grp", "req", "hid"), None, "kv"),
        P(("grp", "req", "hid"), None, "kv"),
        P(("grp", "req", "hid"), None, "kv"),
        P(("grp", "req", "hid"), None, "kv"),
        P(("grp", "req", "hid"), None, "kv"),
        P(("grp", "req", "hid")),
        P(("grp", "req", "hid")),
        P(("grp", "req", "hid"), None, None),
        P(("grp", "req", "hid", "kv"), None),
        P(),
        P(),
        P("kv", ("req", "hid")),
        P("kv", ("req", "hid")),
        P(("req", "hid"), "kv"),
    )
    one_shard_per_expert = mesh.shape["req"] == EXPERTS and mesh.shape["hid"] == 2
    return jax.shard_map(
        local_kernel if one_shard_per_expert and mesh.shape["kv"] == 2 else local,
        mesh=mesh,
        in_specs=placed,
        out_specs=(P(("grp", "req", "hid", "kv"), None), P(("grp", "req", "hid", "kv"), None)),
        check_vma=False,
    )
```

```python
import math

import jax
import jax.numpy as jnp
from jax import lax
from jax.experimental import pallas as pl
from jax.experimental.pallas import tpu as pltpu
from jax.sharding import PartitionSpec as P

HEAD_SIZE = 128
EXPERTS = 4


def attend_request(
    query_rows,
    tree_key_rows,
    tree_value_rows,
    cache_key_rows,
    cache_value_rows,
    length,
    tree_size,
    mask_r,
):
    tree_len = query_rows.shape[0]
    cache_len = cache_key_rows.shape[0]
    kv_heads = cache_key_rows.shape[1] // HEAD_SIZE
    query_count = query_rows.shape[1] // HEAD_SIZE
    heads_per_group = query_count // kv_heads
    query_head_count = query_rows.reshape(tree_len, kv_heads, heads_per_group, HEAD_SIZE)
    cache_key_block = cache_key_rows.reshape(cache_len, kv_heads, HEAD_SIZE)
    cache_value_block = cache_value_rows.reshape(cache_len, kv_heads, HEAD_SIZE)
    tree_key_block = tree_key_rows.reshape(tree_len, kv_heads, HEAD_SIZE)
    tree_value_block = tree_value_rows.reshape(tree_len, kv_heads, HEAD_SIZE)
    scale = 1.0 / math.sqrt(HEAD_SIZE)
    cache_scores = (
        jnp.einsum(
            "tgqd,cgd->gqtc", query_head_count, cache_key_block, preferred_element_type=jnp.float32
        )
        * scale
    )
    tree_scores = (
        jnp.einsum(
            "tgqd,ugd->gqtu", query_head_count, tree_key_block, preferred_element_type=jnp.float32
        )
        * scale
    )
    cache_live = jnp.arange(cache_len, dtype=jnp.int32) < length
    tree_live = (mask_r > 0) & (jnp.arange(tree_len, dtype=jnp.int32)[None, :] < tree_size)
    cache_scores = jnp.where(cache_live[None, None, None, :], cache_scores, -1e30)
    tree_scores = jnp.where(tree_live[None, None], tree_scores, -1e30)
    highest = jnp.maximum(cache_scores.max(-1), tree_scores.max(-1))
    cache_exp = jnp.exp(cache_scores - highest[..., None])
    tree_exp = jnp.exp(tree_scores - highest[..., None])
    summed = cache_exp.sum(-1) + tree_exp.sum(-1)
    cache_prob = (cache_exp / summed[..., None]).astype(jnp.bfloat16)
    tree_prob = (tree_exp / summed[..., None]).astype(jnp.bfloat16)
    output = jnp.einsum(
        "gqtc,cgd->tgqd", cache_prob, cache_value_block, preferred_element_type=jnp.float32
    )
    output = output + jnp.einsum(
        "gqtu,ugd->tgqd", tree_prob, tree_value_block, preferred_element_type=jnp.float32
    )
    return output.reshape(tree_len, query_count * HEAD_SIZE).astype(jnp.bfloat16)


def place_rows(route_block, capacity):
    flat_routes = route_block.reshape(-1)
    onehot = (flat_routes[:, None] == jnp.arange(EXPERTS, dtype=jnp.int32)[None, :]).astype(
        jnp.int32
    )
    before = jnp.cumsum(onehot, axis=0) - onehot
    position = jnp.sum(before * onehot, axis=1)
    return flat_routes * capacity + position


def local(
    residual,
    queries,
    tree_row_keys,
    tree_row_values,
    cache_keys,
    stored_values,
    cache_lengths,
    tree_sizes,
    tree_mask,
    routes,
    norm_gain,
    router,
    gate_weight,
    up_weight,
    down_weight,
):
    attended = jax.vmap(attend_request)(
        queries,
        tree_row_keys,
        tree_row_values,
        cache_keys,
        stored_values,
        cache_lengths,
        tree_sizes,
        tree_mask,
    )
    head_rows = attended.reshape(-1, attended.shape[-1])
    own_rows = lax.all_to_all(head_rows, "kv", split_axis=0, concat_axis=1, tiled=True)
    stream = residual.astype(jnp.float32) + own_rows.astype(jnp.float32)
    normed = (
        stream
        * lax.rsqrt(jnp.mean(stream * stream, axis=-1, keepdims=True) + 1e-05)
        * norm_gain.astype(jnp.float32)
    ).astype(jnp.bfloat16)
    row_count = normed.shape[0]
    width = normed.shape[1]
    capacity = row_count * 2 // EXPERTS + max(1, row_count // 8)
    targets = place_rows(routes, capacity)
    picker = (jnp.arange(EXPERTS * capacity, dtype=jnp.int32)[:, None] == targets[None, :]).astype(
        jnp.bfloat16
    )
    blocks = jnp.dot(
        picker, jnp.repeat(normed, 2, axis=0), preferred_element_type=jnp.float32
    ).astype(jnp.bfloat16)
    gate_full, up_full, down_full = (
        lax.all_gather(gate_weight, "kv", axis=0, tiled=True),
        lax.all_gather(up_weight, "kv", axis=0, tiled=True),
        lax.all_gather(down_weight, "kv", axis=1, tiled=True),
    )
    req_count = lax.axis_size("req")
    group_size = req_count // EXPERTS
    outgoing = jnp.repeat(blocks.reshape(EXPERTS, capacity, width), group_size, axis=0)
    arrived = lax.all_to_all(outgoing, "req", split_axis=0, concat_axis=0, tiled=True)
    inputs = lax.all_gather(arrived.reshape(-1, width), "hid", axis=0, tiled=True)
    gate = jnp.dot(inputs, gate_full, preferred_element_type=jnp.float32)
    up_part = jnp.dot(inputs, up_full, preferred_element_type=jnp.float32)
    hidden = (jax.nn.silu(gate) * up_part).astype(jnp.bfloat16)
    partial_out = jnp.dot(hidden, down_full, preferred_element_type=jnp.float32)
    reduced = lax.psum_scatter(
        partial_out.astype(jnp.bfloat16), "hid", scatter_dimension=0, tiled=True
    ).astype(jnp.float32)
    returned = lax.all_to_all(
        reduced.reshape(req_count, capacity, width).astype(jnp.bfloat16),
        "req",
        split_axis=0,
        concat_axis=0,
        tiled=True,
    ).astype(jnp.float32)
    expert_sums = (
        returned.reshape(EXPERTS, group_size, capacity, width)
        .sum(axis=1)
        .reshape(EXPERTS * capacity, width)
    )
    picked = expert_sums[targets].reshape(row_count, 2, width)
    logits = jnp.dot(normed, router, preferred_element_type=jnp.float32)
    chosen = jnp.take_along_axis(logits, routes, axis=1)
    gates = jax.nn.softmax(chosen, axis=-1)
    mixture = jnp.sum(gates[:, :, None] * picked, axis=1)
    return (mixture.astype(jnp.bfloat16), (stream + mixture).astype(jnp.bfloat16))


WAYS = 2
OUT_TILES = 2
MESH = pl.DeviceIdType.MESH
FAR = (1, 3, 2)


def layer_kernel(
    len_ref, tsz_ref, res_ref, q_ref, tk_ref, tv_ref, mask_ref, routes_ref, gain_ref, router_ref,
    ck_hbm, cv_hbm, wg_hbm, wu_hbm, wd_hbm,
    out_ref,
    ck, cv, wg, wu, wd,
    xs, xr, sq_s, sq_r, lg_s, lg_r, gates_ref, stream_ref, rows,
    ps, pr, hidden, acc_ref, own_ref, half_s, half_r, summed, back, mixf, hidf, fin_s, fin_r,
    kv_sem, wg_sem, wu_sem, wd_sem, tiny_s, tiny_r, row_zs, row_xs, row_r,
    ps_s, ps_r, h_s, h_r, half_ss, half_rs, back_s, back_r,
):
    req, hid, kv = lax.axis_index("req"), lax.axis_index("hid"), lax.axis_index("kv")
    n_req = rows.shape[0] // 2
    t_rows, half = rows.shape[1], rows.shape[2]
    piece = wg.shape[2]
    tile = wd.shape[2]
    o_rows = res_ref.shape[0]
    okv, ohid = 1 - kv, 1 - hid
    bf, f32 = jnp.bfloat16, jnp.float32
    peer_kv, peer_hid = {"kv": okv}, {"hid": ohid}

    def remote(src, dst, ss, rs, dev):
        return pltpu.make_async_remote_copy(
            src_ref=src, dst_ref=dst, send_sem=ss, recv_sem=rs, device_id=dev, device_id_type=MESH
        )

    copy_k = pltpu.make_async_copy(ck_hbm.at[0], ck, kv_sem.at[0])
    copy_v = pltpu.make_async_copy(cv_hbm.at[0], cv, kv_sem.at[1])
    copy_k.start()
    copy_v.start()

    def weight_copy(which, c):
        hbm, ref, sem = ((wg_hbm, wg, wg_sem), (wu_hbm, wu, wu_sem))[which]
        return pltpu.make_async_copy(
            hbm.at[:, pl.ds(pl.multiple_of(c * piece, piece), piece)], ref.at[c], sem.at[c]
        )

    def down_copy(n):
        return pltpu.make_async_copy(wd_hbm.at[:, pl.ds(n * tile, tile)], wd.at[n], wd_sem.at[n])


    barrier = pltpu.get_barrier_semaphore()
    others = [lax.rem(req + d, n_req) for d in FAR]
    for dev in [peer_kv, peer_hid] + [{"req": z} for z in others]:
        pl.semaphore_signal(barrier, inc=1, device_id=dev, device_id_type=MESH)

    scale = 1.0 / math.sqrt(HEAD_SIZE)
    groups = ck.shape[1] // HEAD_SIZE
    per = half // HEAD_SIZE // groups
    length, tsz = len_ref[0], tsz_ref[0]
    mask = mask_ref[0]
    mask = jnp.concatenate([mask] * per, axis=0)
    tree_live = (mask > 0) & (lax.broadcasted_iota(jnp.int32, mask.shape, 1) < tsz)
    slots = ck.shape[0]
    live = lax.broadcasted_iota(jnp.int32, (1, slots), 1) < length
    nt = (((1,), (1,)), ((), ()))
    copy_k.wait()
    heads = []
    scores = []
    for g in range(groups):
        cols = slice(g * HEAD_SIZE, (g + 1) * HEAD_SIZE)
        q = jnp.concatenate(
            [q_ref[0, :, (g * per + j) * HEAD_SIZE : (g * per + j + 1) * HEAD_SIZE] for j in range(per)],
            axis=0,
        )
        s = lax.dot_general(q, ck[:, cols], nt, preferred_element_type=f32) * scale
        t = lax.dot_general(q, tk_ref[0, :, cols], nt, preferred_element_type=f32) * scale
        scores.append((jnp.where(live, s, -1e30), jnp.where(tree_live, t, -1e30)))
    pl.semaphore_wait(barrier, 2 + len(others))

    lane = lax.broadcasted_iota(jnp.int32, (o_rows, 128), 1)
    routes = routes_ref[...].astype(f32)
    square = (o_rows, o_rows)
    diagonal = lax.broadcasted_iota(jnp.int32, square, 0) == lax.broadcasted_iota(jnp.int32, square, 1)
    choice = [
        jnp.sum(jnp.where(diagonal, routes[k : k + 1, :], 0.0), axis=1, keepdims=True) for k in range(2)
    ]
    route_lanes = jnp.where(lane == 0, choice[0], jnp.where(lane == 1, choice[1], 0.0))
    xs[:, :half] = res_ref[:, pl.ds(pl.multiple_of(okv * half, half), half)].astype(f32)
    xs[:, half:] = route_lanes
    swap = remote(xs, xr.at[kv], tiny_s.at[0], tiny_r.at[0], peer_kv)
    swap.start()
    xr[kv, :, :half] = res_ref[:, pl.ds(pl.multiple_of(kv * half, half), half)].astype(f32)
    xr[kv, :, half:] = route_lanes

    copy_v.wait()
    for base in (okv, kv):
        for c in range(WAYS):
            weight_copy(0, base * WAYS + c).start()
            weight_copy(1, base * WAYS + c).start()
    for g in range(groups):
        cols = slice(g * HEAD_SIZE, (g + 1) * HEAD_SIZE)
        s, t = scores[g]
        top = jnp.maximum(s.max(-1, keepdims=True), t.max(-1, keepdims=True))
        s, t = jnp.exp(s - top), jnp.exp(t - top)
        inv = 1.0 / (s.sum(-1, keepdims=True) + t.sum(-1, keepdims=True))
        o = jnp.dot((s * inv).astype(bf), cv[:, cols], preferred_element_type=f32)
        o = o + jnp.dot((t * inv).astype(bf), tv_ref[0, :, cols], preferred_element_type=f32)
        o = o.astype(bf).astype(f32)
        heads += [o[j * t_rows : (j + 1) * t_rows] for j in range(per)]
    attn = jnp.concatenate(heads, axis=1)

    remote(xs, xr.at[okv], tiny_s.at[0], tiny_r.at[0], peer_kv).wait_recv()
    both = xr[...].reshape(t_rows, half + 128)
    stream = both[:, :half] + attn
    stream_ref[...] = stream
    sq_s[...] = jnp.broadcast_to(jnp.sum(stream * stream, axis=-1, keepdims=True), sq_s.shape)
    swap_sq = remote(sq_s, sq_r, tiny_s.at[1], tiny_r.at[1], peer_kv)
    swap_sq.start()
    gain = gain_ref[...].astype(f32)
    strips = half // 128
    gain = jnp.where(kv == 0, gain[:strips], gain[strips:])
    gained = jnp.concatenate([gain[j : j + 1] for j in range(strips)], axis=1)
    swap_sq.wait_recv()
    mean = (sq_s[:, 0:1] + sq_r[:, 0:1]) * (1.0 / (2 * half))
    normed = (stream * lax.rsqrt(mean + 1e-05) * gained).astype(bf)

    me = hid * n_req + req
    rows[me] = normed
    sends = [remote(rows.at[me], rows.at[me], row_xs.at[0], row_r.at[me], peer_hid)]
    for d, z in enumerate(others):
        sends.append(remote(rows.at[me], rows.at[me], row_zs.at[d], row_r.at[me], {"req": z}))
    for copy in sends:
        copy.start()

    normed = normed.astype(f32)
    router = router_ref[:, pl.ds(pl.multiple_of(kv * half, half), half)].astype(f32)
    lanes = lax.broadcasted_iota(jnp.int32, (t_rows, 128), 1)
    part = jnp.zeros((t_rows, 128), f32)
    for e in range(EXPERTS):
        one = jnp.sum(normed * router[e : e + 1, :], axis=-1, keepdims=True)
        part = jnp.where(lanes == e, one, part)
    lg_s[...] = part
    swap_lg = remote(lg_s, lg_r, tiny_s.at[2], tiny_r.at[2], peer_kv)
    swap_lg.start()

    def wait_rows(slot):
        remote(rows.at[slot], rows.at[slot], row_xs.at[0], row_r.at[slot], peer_hid).wait_recv()

    for d, z in enumerate(others):
        slot = hid * n_req + z
        wait_rows(slot)
        copy = remote(rows.at[slot], rows.at[slot], row_xs.at[d + 1], row_r.at[slot], peer_hid)
        copy.start()
        sends.append(copy)

    swap_lg.wait_recv()
    logits = lg_s[...] + lg_r[...]
    lane_f = lanes.astype(f32)
    first, second = both[:, half : half + 1], both[:, half + 1 : half + 2]
    is_first, is_second = lane_f == first, lane_f == second
    a = jnp.sum(jnp.where(is_first, logits, 0.0), axis=-1, keepdims=True)
    b = jnp.sum(jnp.where(is_second, logits, 0.0), axis=-1, keepdims=True)
    ab = jnp.maximum(a, b)
    ea, eb = jnp.exp(a - ab), jnp.exp(b - ab)
    gates_ref[...] = jnp.where(is_first, ea / (ea + eb), jnp.where(is_second, eb / (ea + eb), 0.0))

    for z in range(n_req):
        wait_rows(ohid * n_req + lax.rem(req + z, n_req))

    for n in range(OUT_TILES):
        down_copy(n).start()
    count = 2 * n_req * t_rows

    def both_dots(c):
        weight_copy(0, c).wait()
        weight_copy(1, c).wait()
        x = rows[...].reshape(count, half)
        return (
            jnp.dot(x, wg[c], preferred_element_type=f32),
            jnp.dot(x, wu[c], preferred_element_type=f32),
        )

    def pair_copy(c):
        return remote(ps.at[c], pr.at[c], ps_s.at[c], ps_r.at[c], peer_kv)

    def hidden_copy(which, c):
        view = hidden.at[which, :, pl.ds(pl.multiple_of(c * piece, piece), piece)]
        return remote(view, view, h_s.at[c], h_r.at[c], peer_kv)

    def partner_step(c, _):
        gate, up = both_dots(okv * WAYS + c)
        ps[c, 0] = gate.astype(bf)
        ps[c, 1] = up.astype(bf)
        pair_copy(c).start()
        return 0

    lax.fori_loop(0, WAYS, partner_step, 0)

    def own_step(c, _):
        gate, up = both_dots(kv * WAYS + c)
        pair_copy(c).wait_recv()
        gate = gate + pr[c, 0].astype(f32)
        up = up + pr[c, 1].astype(f32)
        value = (gate / (1.0 + jnp.exp(-gate)) * up).astype(bf)
        hidden[kv, :, pl.ds(pl.multiple_of(c * piece, piece), piece)] = value
        hidden_copy(kv, c).start()
        return 0

    lax.fori_loop(0, WAYS, own_step, 0)

    span = WAYS * piece

    def down_dot(which, n):
        return jnp.dot(
            hidden[which],
            wd[n, pl.ds(pl.multiple_of(which * span, span), span), :],
            preferred_element_type=f32,
        )

    def half_copy(n):
        return remote(half_s.at[n], half_r.at[n], half_ss.at[n], half_rs.at[n], peer_hid)

    def back_copy(n, d, z):
        return remote(
            summed.at[n, z], back.at[n, req], back_s.at[n, d], back_r.at[n, req], {"req": z}
        )

    def forward(n):
        half_copy(n).wait_recv()
        total = (own_ref[n] + half_r[n].astype(f32)).astype(bf)
        summed[n] = total.reshape(n_req, t_rows, tile)
        for d, z in enumerate(others):
            back_copy(n, d, z).start()
        back[n, req] = summed[n, req]

    def down_step(n, _):
        down_copy(n).wait()
        acc_ref[...] = down_dot(kv, n).reshape(acc_ref.shape)

        @pl.when(n == 0)
        def _():
            for c in range(WAYS):
                hidden_copy(okv, c).wait_recv()

        acc_ref[...] += down_dot(okv, n).reshape(acc_ref.shape)
        half_s[n] = acc_ref[ohid].astype(bf)
        half_copy(n).start()
        own_ref[n] = acc_ref[hid]

        @pl.when(n > 0)
        def _():
            forward(n - 1)

        return 0

    lax.fori_loop(0, OUT_TILES, down_step, 0)
    forward(OUT_TILES - 1)

    gates = gates_ref[...]
    for n in range(OUT_TILES):
        for z in others:
            remote(
                summed.at[n, z], back.at[n, z], back_s.at[n, 0], back_r.at[n, z], {"req": z}
            ).wait_recv()
        mix = jnp.zeros((t_rows, tile), f32)
        for e in range(EXPERTS):
            mix = mix + gates[:, e : e + 1] * back[n, e].astype(f32)
        cols = slice(n * tile, (n + 1) * tile)
        mixf[:, :, cols] = mix.reshape(2, o_rows, tile)
        hidf[:, :, cols] = (stream_ref[:, cols] + mix).reshape(2, o_rows, tile)

    fin_s[...] = jnp.concatenate([mixf[okv], hidf[okv]], axis=0).astype(bf)
    last = remote(fin_s, fin_r, tiny_s.at[3], tiny_r.at[3], peer_kv)
    last.start()
    mine = pl.ds(pl.multiple_of(kv * half, half), half)
    out_ref[:, mine] = jnp.concatenate([mixf[kv], hidf[kv]], axis=0).astype(bf)
    last.wait_recv()
    theirs = pl.ds(pl.multiple_of(okv * half, half), half)
    out_ref[:, theirs] = fin_r[...]

    for copy in [swap, swap_sq, swap_lg, last] + sends:
        copy.wait_send()
    for c in range(WAYS):
        pair_copy(c).wait_send()
        hidden_copy(kv, c).wait_send()
    for n in range(OUT_TILES):
        half_copy(n).wait_send()
        for d, z in enumerate(others):
            back_copy(n, d, z).wait_send()


def local_kernel(
    residual, queries, tree_row_keys, tree_row_values, cache_keys, stored_values, cache_lengths,
    tree_sizes, tree_mask, routes, norm_gain, router, gate_weight, up_weight, down_weight,
):
    bf, f32 = jnp.bfloat16, jnp.float32
    n_req = lax.axis_size("req")
    o_rows, width = residual.shape
    half = width // 2
    t_rows = queries.shape[1]
    slots, kv_cols = cache_keys.shape[1:]
    units = gate_weight.shape[1]
    piece = units // 2 // WAYS
    tile = half // OUT_TILES
    count = 2 * n_req * t_rows
    side = n_req * t_rows
    vm = pl.BlockSpec(memory_space=pltpu.VMEM)
    sm = pl.BlockSpec(memory_space=pltpu.SMEM)
    hb = pl.BlockSpec(memory_space=pl.ANY)
    dma = pltpu.SemaphoreType.DMA
    scratch = [
        pltpu.VMEM((slots, kv_cols), bf),
        pltpu.VMEM((slots, kv_cols), bf),
        pltpu.VMEM((2 * WAYS, half, piece), bf),
        pltpu.VMEM((2 * WAYS, half, piece), bf),
        pltpu.VMEM((OUT_TILES, units, tile), bf),
        pltpu.VMEM((o_rows, half + 128), f32),
        pltpu.VMEM((2, o_rows, half + 128), f32),
        pltpu.VMEM((t_rows, 128), f32),
        pltpu.VMEM((t_rows, 128), f32),
        pltpu.VMEM((t_rows, 128), f32),
        pltpu.VMEM((t_rows, 128), f32),
        pltpu.VMEM((t_rows, 128), f32),
        pltpu.VMEM((t_rows, half), f32),
        pltpu.VMEM((2 * n_req, t_rows, half), bf),
        pltpu.VMEM((WAYS, 2, count, piece), bf),
        pltpu.VMEM((WAYS, 2, count, piece), bf),
        pltpu.VMEM((2, count, units // 2), bf),
        pltpu.VMEM((2, side, tile), f32),
        pltpu.VMEM((OUT_TILES, side, tile), f32),
        pltpu.VMEM((OUT_TILES, side, tile), bf),
        pltpu.VMEM((OUT_TILES, side, tile), bf),
        pltpu.VMEM((OUT_TILES, n_req, t_rows, tile), bf),
        pltpu.VMEM((OUT_TILES, n_req, t_rows, tile), bf),
        pltpu.VMEM((2, o_rows, half), f32),
        pltpu.VMEM((2, o_rows, half), f32),
        pltpu.VMEM((t_rows, half), bf),
        pltpu.VMEM((t_rows, half), bf),
        dma((2,)), dma((2 * WAYS,)), dma((2 * WAYS,)), dma((OUT_TILES,)),
        dma((4,)), dma((4,)),
        dma((n_req - 1,)), dma((n_req,)), dma((2 * n_req,)),
        dma((WAYS,)), dma((WAYS,)), dma((WAYS,)), dma((WAYS,)),
        dma((OUT_TILES,)), dma((OUT_TILES,)),
        dma((OUT_TILES, n_req - 1)), dma((OUT_TILES, n_req)),
    ]
    both = pl.pallas_call(
        layer_kernel,
        out_shape=jax.ShapeDtypeStruct((2 * o_rows, width), bf),
        in_specs=[sm, sm] + [vm] * 8 + [hb] * 5,
        out_specs=vm,
        scratch_shapes=scratch,
        compiler_params=pltpu.CompilerParams(
            collective_id=0, has_side_effects=True, vmem_limit_bytes=58 * 1024 * 1024
        ),
        cost_estimate=pl.CostEstimate(
            flops=6 * count * half * units, bytes_accessed=6 * half * units, transcendentals=0
        ),
    )(
        cache_lengths, tree_sizes, residual, queries, tree_row_keys, tree_row_values, tree_mask,
        routes.T, norm_gain.reshape(-1, 128), router.T,
        cache_keys, stored_values, gate_weight, up_weight, down_weight,
    )
    return both[:o_rows], both[o_rows:]


def solution(mesh):
    placed = (
        P(("grp", "req", "hid", "kv"), None),
        P(("grp", "req", "hid"), None, "kv"),
        P(("grp", "req", "hid"), None, "kv"),
        P(("grp", "req", "hid"), None, "kv"),
        P(("grp", "req", "hid"), None, "kv"),
        P(("grp", "req", "hid"), None, "kv"),
        P(("grp", "req", "hid")),
        P(("grp", "req", "hid")),
        P(("grp", "req", "hid"), None, None),
        P(("grp", "req", "hid", "kv"), None),
        P(),
        P(),
        P("kv", ("req", "hid")),
        P("kv", ("req", "hid")),
        P(("req", "hid"), "kv"),
    )
    one_shard_per_expert = mesh.shape["req"] == EXPERTS and mesh.shape["hid"] == 2
    return jax.shard_map(
        local_kernel if one_shard_per_expert and mesh.shape["kv"] == 2 else local,
        mesh=mesh,
        in_specs=placed,
        out_specs=(P(("grp", "req", "hid", "kv"), None), P(("grp", "req", "hid", "kv"), None)),
        check_vma=False,
    )
```
